32 devices in a mesh: depth: 8 (over y, x, core), freq: 4 (over z).
Axes of the slice: x: 2, y: 2, z: 4, core: 2. Of those that a mesh axis runs over, the one named last changes fastest.
Arguments:
- source_field: float32 [4, 2, 64, 2048], P('freq'), may hold values from -6 to 6
- receiver_data: float32 [4, 2, 64, 2048], P('freq'), may hold values from -6 to 6
- propagator: bfloat16 [4, 8, 16, 6, 2, 128, 128], P('freq', 'depth'), may hold values from -0.102062073 to 0.102062073
- block_columns: int32 [8, 16, 6], P('depth'), may hold values from 0 to 15, as said below
- image_pairs: int32 [8, 8, 2], P('depth'), may hold values from 0 to 15, as said below
Outputs:
- image: float32 [8, 8, 128, 128], P('depth', 'freq')
The draws below stay inside these ranges and needn't reach their ends.
Inputs may be any that keep to these rules, and one draw needn't show every extreme that they name: `block_columns`: each block row lists 6 distinct block columns, its own among them. `image_pairs`: the two block indices of a pair differ by at most one.
All inputs are finite; a program needn't handle non-finite values.
Results may differ from the reference program's by a relative error of at most 0.0003.
Values sent between devices are 32-bit elements; how exact they have to be, the bound alone decides.
No kernel may reach another device: no remote copies, remote signals or barrier semaphores. Data moves between devices by JAX's collectives and lax.ppermute only.
A program may use at most 64 MiB of HBM per device.

```python
import math
import jax
import jax.numpy as jnp
from jax import lax

X = 2048
BLOCK = 128
NNZ = 6
NBR = 16
SHOTS = 64
LEVELS = 8
FREQS = 4
NI = 8


def surface_values(key):
    shape = (FREQS, 2, SHOTS, X)
    values = jnp.clip(jax.random.normal(key, shape, jnp.float32), -6.0, 6.0)
    return values.astype(jnp.float32)


def draw_source_field(key, part):
    return surface_values(jax.random.fold_in(key, 21))


def draw_receiver_data(key, part):
    return surface_values(jax.random.fold_in(key, 22))


def draw_propagator(key, part):
    own_key = jax.random.fold_in(key, 23)
    spread = 1.0 / math.sqrt(2.0 * NNZ * BLOCK)
    shape = (FREQS, LEVELS, NBR, NNZ, 2, BLOCK, BLOCK)
    values = jnp.clip(jax.random.normal(own_key, shape, jnp.float32), -4.0, 4.0)
    return (values * spread).astype(jnp.bfloat16)


def draw_block_columns(key, part):
    scores = jax.random.randint(key, (LEVELS, NBR, NBR), 0, 1 << 20)
    columns = jnp.arange(NBR, dtype=jnp.int32)
    scores = scores * NBR + columns[None, None, :]
    diagonal = columns[:, None] == columns[None, :]
    scores = jnp.where(diagonal[None], (1 << 20) * NBR + NBR, scores)
    unused, picked = lax.top_k(scores, NNZ)
    return picked.astype(jnp.int32)


def draw_image_pairs(key, part):
    key_rows = jax.random.fold_in(key, 11)
    key_step = jax.random.fold_in(key, 12)
    key_first = jax.random.fold_in(key, 13)
    key_second = jax.random.fold_in(key, 14)
    block_rows = jax.random.randint(key_rows, (LEVELS, NI), 0, NBR)
    slots = jnp.arange(NI, dtype=jnp.int32)[None, :]
    first_slot = jax.random.randint(key_first, (LEVELS, 1), 0, NI)
    second_slot = (first_slot + 1 + jax.random.randint(key_second, (LEVELS, 1), 0, NI - 1)) % NI
    block_rows = jnp.where(slots == first_slot, 0, jnp.where(slots == second_slot, NBR - 1, block_rows))
    offsets = jax.random.randint(key_step, (LEVELS, NI), -1, 2)
    block_cols = jnp.clip(block_rows + offsets, 0, NBR - 1)
    return jnp.stack([block_rows, block_cols], axis=-1).astype(jnp.int32)


def setup_inputs(seed: int = 0) -> dict:
    arg_keys = jax.random.split(jax.random.key(seed), 6)
    source_field = draw_source_field(jax.random.fold_in(arg_keys[5], 71), 0)
    receiver_data = draw_receiver_data(jax.random.fold_in(arg_keys[5], 71), 0)
    propagator = draw_propagator(jax.random.fold_in(arg_keys[5], 71), 0)
    block_columns = draw_block_columns(jax.random.fold_in(arg_keys[5], 71), 0)
    image_pairs = draw_image_pairs(jax.random.fold_in(arg_keys[5], 71), 0)
    return {"source_field": source_field, "receiver_data": receiver_data, "propagator": propagator, "block_columns": block_columns, "image_pairs": image_pairs}


def edge_taper(lateral):
    position = jnp.arange(lateral, dtype=jnp.int32)
    distance = jnp.minimum(position, lateral - 1 - position).astype(jnp.float32)
    edge_cells = lateral // 32
    edge_ramp = jnp.maximum(0.0, 1.0 - distance / edge_cells)
    return 1.0 - 0.3 * edge_ramp * edge_ramp

def propagate(field, level_operator, level_columns, taper_row):
    lane_count, shot_count, lateral = field.shape
    block_rows = level_columns.shape[0]
    blocks = field.reshape(lane_count, shot_count, block_rows, lateral // block_rows)
    picked = jnp.take(blocks, level_columns, axis=2)
    operator_real = level_operator[:, :, 0].astype(jnp.float32)
    operator_imag = level_operator[:, :, 1].astype(jnp.float32)
    real_part = jnp.einsum('cbrjk,rjkm->cbrm', picked, operator_real, precision=lax.Precision.HIGHEST)
    imag_part = jnp.einsum('cbrjk,rjkm->cbrm', picked, operator_imag, precision=lax.Precision.HIGHEST)
    source_real = real_part[0] - imag_part[1]
    source_imag = real_part[1] + imag_part[0]
    receiver_real = real_part[2] + imag_part[3]
    receiver_imag = real_part[3] - imag_part[2]
    combined = jnp.stack([source_real, source_imag, receiver_real, receiver_imag])
    return combined.reshape(lane_count, shot_count, lateral) * taper_row

def image_level(field, level_pairs):
    lane_count, shot_count, lateral = field.shape
    block_size = lateral // (lateral // BLOCK)
    blocks = field.reshape(lane_count, shot_count, lateral // block_size, block_size)
    source_blocks = jnp.take(blocks[0:2], level_pairs[:, 0], axis=2)
    receiver_blocks = jnp.take(blocks[2:4], level_pairs[:, 1], axis=2)
    return jnp.einsum('csik,csim->ikm', source_blocks, receiver_blocks, precision=lax.Precision.HIGHEST)

def reference(source_field, receiver_data, propagator, block_columns, image_pairs):
    taper_row = edge_taper(X)
    surface = jnp.concatenate([source_field, receiver_data], axis=1).astype(jnp.float32)
    image_scale = 1.0 / math.sqrt(2.0 * SHOTS * FREQS)

    def one_level(wavefield, level_index):
        level_operator = lax.dynamic_index_in_dim(propagator, level_index, 1, keepdims=False)
        level_columns = lax.dynamic_index_in_dim(block_columns, level_index, 0, keepdims=False)
        level_pairs = lax.dynamic_index_in_dim(image_pairs, level_index, 0, keepdims=False)
        advanced = jax.vmap(propagate, in_axes=(0, 0, None, None))(wavefield, level_operator, level_columns, taper_row)
        level_image = lax.optimization_barrier(jnp.sum(jax.vmap(image_level, in_axes=(0, None))(advanced, level_pairs), axis=0))
        return (advanced, level_image * image_scale)
    unused, image = lax.scan(one_level, surface, jnp.arange(LEVELS, dtype=jnp.int32))
    return image
```

```python
import functools
import math

import jax
import jax.numpy as jnp
from jax import lax
from jax.experimental import pallas as pl
from jax.experimental.pallas import tpu as pltpu
from jax.sharding import PartitionSpec as P

GROUPS = 4
NEAR_DELAY = 1
FAR_DELAY = 2
UNROLL = 16
SMEM = pl.BlockSpec(memory_space=pltpu.SMEM)
VMEM = pl.BlockSpec(memory_space=pltpu.VMEM)
HBM = pl.BlockSpec(memory_space=pltpu.HBM)


def edge_taper(lateral):
    position = jnp.arange(lateral, dtype=jnp.int32)
    distance = jnp.minimum(position, lateral - 1 - position).astype(jnp.float32)
    edge_cells = lateral // 32
    edge_ramp = jnp.maximum(0.0, 1.0 - distance / edge_cells)
    return 1.0 - 0.3 * edge_ramp * edge_ramp


def split_halves(value):
    high = value.astype(jnp.bfloat16)
    low = (value - high.astype(jnp.float32)).astype(jnp.bfloat16)
    return high, low


def load_kernel(columns, pairs, taper, operator, out, semaphore):
    copy = pltpu.make_async_copy(operator.at[0, 0], out, semaphore)
    copy.start()
    copy.wait()


def entry_turn(depth):
    return (depth + 1) // 2 * NEAR_DELAY + depth // 2 * FAR_DELAY


def propagate_kernel(*refs, turn, first_shot, near_in, far_in, surface_in):
    refs = list(refs)
    columns, operator, taper, kept_in = refs[:4]
    del refs[:4]
    depth = lax.axis_index("depth")
    group = turn - entry_turn(depth)
    active = jnp.logical_and(group >= 0, group < GROUPS)
    odd = lax.rem(depth, 2) == 1
    near = refs.pop(0) if near_in else None
    far = refs.pop(0) if far_in else None
    surface = [refs.pop(0), refs.pop(0)] if surface_in else None
    out, kept, split = refs[:3]
    block_rows, nnz = operator.shape[0], operator.shape[1]
    width = operator.shape[-1]
    rows = out.shape[2]
    shots = rows // 2

    def put(block, part, value):
        high, low = split_halves(value)
        split[block, part * rows:(part + 1) * rows, :] = high
        split[block, (2 + part) * rows:(3 + part) * rows, :] = low

    def take(field):
        for block in range(block_rows):
            for part in range(2):
                put(block, part, field[block, part])

    if surface_in:
        drawn, semaphores = refs[3:5]

        @pl.when(jnp.logical_and(active, depth == 0))
        def _():
            copies = [
                pltpu.make_async_copy(
                    surface[k].at[0, :, pl.ds(first_shot, shots), :],
                    drawn.at[k], semaphores.at[k])
                for k in range(2)
            ]
            for copy in copies:
                copy.start()
            for copy in copies:
                copy.wait()
            for block in range(block_rows):
                lanes = slice(block * width, (block + 1) * width)
                for part in range(2):
                    receiver = drawn[1, part, :, lanes]
                    if part == 1:
                        receiver = -receiver
                    put(block, part, jnp.concatenate([drawn[0, part, :, lanes], receiver], axis=0))

    if near_in:
        @pl.when(jnp.logical_and(active, odd))
        def _():
            take(near)

    if far_in:
        @pl.when(jnp.logical_and(active, jnp.logical_and(depth > 0, jnp.logical_not(odd))))
        def _():
            take(far)

    @pl.when(active)
    def _():
        def one_row(r, carry):
            picked = jnp.concatenate(
                [split[columns[r * nnz + j]] for j in range(nnz)], axis=1
            )
            real = operator[r, :, 0].reshape(nnz * width, width)
            imag = operator[r, :, 1].reshape(nnz * width, width)
            weights = jnp.concatenate([real, imag], axis=1)
            product = jnp.dot(picked, weights, preferred_element_type=jnp.float32)
            product = product[: 2 * rows] + product[2 * rows:]
            scale = taper[pl.ds(r, 1), :]
            real_out = (product[:rows, :width] - product[rows:, width:]) * scale
            imag_out = (product[rows:, :width] + product[:rows, width:]) * scale
            out[r, 0] = real_out
            out[r, 1] = imag_out
            kept[group, r, 0] = real_out
            kept[group, r, 1] = imag_out
            return carry

        lax.fori_loop(0, block_rows, one_row, 0, unroll=UNROLL)


def image_block(pairs, index, kept, groups, scale):
    shots = kept.shape[3] // 2
    a = pairs[2 * index]
    b = pairs[2 * index + 1]
    left = jnp.concatenate(
        [kept[g, a, part, :shots, :] for g in groups for part in range(2)], axis=0
    ) * scale
    right = jnp.concatenate(
        [kept[g, b, part, shots:, :] * (1.0 - 2.0 * part) for g in groups for part in range(2)],
        axis=0,
    )
    left_high, left_low = split_halves(left)
    right_high, right_low = split_halves(right)
    lhs = jnp.concatenate([left_high, left_high, left_low], axis=0)
    rhs = jnp.concatenate([right_high, right_low, right_high], axis=0)
    return lax.dot_general(
        lhs, rhs, (((0,), (0,)), ((), ())), preferred_element_type=jnp.float32
    )


def early_kernel(pairs, kept_in, kept, out, *, groups, scale):
    for index in range(out.shape[0]):
        out[index] = image_block(pairs, index, kept_in, groups, scale)


def last_kernel(pairs, early, kept, *outs, groups, scale):
    share = outs[0].shape[0]
    parts = len(outs)
    own = lax.axis_index("freq")
    for step in range(parts):
        owner = lax.rem(own + step, parts)
        for index in range(share):
            pair = owner * share + index
            outs[step][index] = early[pair] + image_block(pairs, pair, kept, groups, scale)


def shards(source_field, receiver_data, propagator, block_columns, image_pairs):
    depth_count = lax.axis_size("depth")
    freq_count = lax.axis_size("freq")
    shots_all, lateral = source_field.shape[2:]
    block_rows, nnz = propagator.shape[2:4]
    width = propagator.shape[-1]
    pair_count = image_pairs.shape[1]
    shots = shots_all // GROUPS
    rows = 2 * shots
    taper = edge_taper(lateral).reshape(block_rows, width)
    scale = 1.0 / math.sqrt(2.0 * shots_all * freq_count)
    columns = block_columns[0].reshape(-1)
    pairs = image_pairs[0].reshape(-1)
    field_type = pltpu.VMEM((block_rows, 2, rows, width), jnp.float32)
    kept_type = pltpu.VMEM((GROUPS, block_rows, 2, rows, width), jnp.float32)
    params = pltpu.CompilerParams(vmem_limit_bytes=16 * 1024 * 1024)

    turns = GROUPS + entry_turn(depth_count - 1)

    operator = pl.pallas_call(
        load_kernel,
        out_shape=pltpu.VMEM(propagator.shape[2:], propagator.dtype),
        in_specs=[SMEM, SMEM, VMEM, HBM],
        out_specs=VMEM,
        scratch_shapes=[pltpu.SemaphoreType.DMA],
        compiler_params=params,
    )(columns, pairs, taper, propagator)

    def active(d, turn):
        return 0 <= turn - entry_turn(d) < GROUPS

    def steps(turn, odd):
        return [(d, d + 1) for d in range(depth_count - 1)
                if d % 2 == odd and active(d, turn)]

    kept = None
    early = None
    near_sent = {}
    far_sent = {}
    for turn in range(turns):
        near = near_sent.pop(turn - NEAR_DELAY, None)
        far = far_sent.pop(turn - FAR_DELAY, None)
        surface_in = turn < GROUPS
        operands = [columns, operator, taper]
        specs = [SMEM, VMEM, VMEM]
        if kept is None:
            kept = pl.pallas_call(
                lambda out: None, out_shape=kept_type, out_specs=VMEM, compiler_params=params)()
        operands.append(kept)
        specs.append(VMEM)
        for value in (near, far):
            if value is not None:
                operands.append(value)
                specs.append(VMEM)
        scratch = [pltpu.VMEM((block_rows, 4 * rows, width), jnp.bfloat16)]
        if surface_in:
            operands += [source_field, receiver_data]
            specs += [HBM, HBM]
            scratch += [pltpu.VMEM((2, 2, shots, lateral), jnp.float32),
                        pltpu.SemaphoreType.DMA((2,))]
        field, kept = pl.pallas_call(
            functools.partial(
                propagate_kernel, turn=turn, first_shot=min(turn, GROUPS - 1) * shots,
                near_in=near is not None, far_in=far is not None, surface_in=surface_in),
            out_shape=(field_type, kept_type),
            in_specs=specs,
            out_specs=(VMEM, VMEM),
            input_output_aliases={3: 1},
            scratch_shapes=scratch,
            compiler_params=params,
            cost_estimate=pl.CostEstimate(
                flops=2 * 4 * rows * block_rows * nnz * 2 * width * width,
                bytes_accessed=block_rows * nnz * 4 * width * width, transcendentals=0),
        )(*operands)
        near_steps = steps(turn, 0)
        far_steps = steps(turn, 1)
        if near_steps:
            near_sent[turn] = lax.ppermute(field, "depth", near_steps)
        if far_steps:
            far_sent[turn] = lax.ppermute(field, "depth", far_steps)
        if turn == turns - 2:
            image_type = jax.ShapeDtypeStruct((pair_count, width, width), jnp.float32)
            kept, early = pl.pallas_call(
                functools.partial(early_kernel, groups=list(range(GROUPS - 1)), scale=scale),
                out_shape=(kept_type, image_type),
                in_specs=[SMEM, VMEM],
                out_specs=(VMEM, VMEM),
                input_output_aliases={1: 0},
                compiler_params=params,
            )(pairs, kept)

    share = pair_count // freq_count
    share_type = jax.ShapeDtypeStruct((share, width, width), jnp.float32)
    shares = pl.pallas_call(
        functools.partial(last_kernel, groups=[GROUPS - 1], scale=scale),
        out_shape=(share_type,) * freq_count,
        in_specs=[SMEM, VMEM, VMEM],
        out_specs=(VMEM,) * freq_count,
        compiler_params=params,
    )(pairs, early, kept)
    total = shares[0]
    for step in range(1, freq_count):
        total += lax.ppermute(
            shares[step], "freq", [(f, (f + step) % freq_count) for f in range(freq_count)])
    return total[None]


def solution(mesh):
    placed = (
        P("freq", None, None, None),
        P("freq", None, None, None),
        P("freq", "depth", None, None, None, None, None),
        P("depth", None, None),
        P("depth", None, None),
    )
    return jax.shard_map(
        shards,
        mesh=mesh,
        in_specs=placed,
        out_specs=P("depth", "freq", None, None),
        check_vma=False,
    )
```

```python
import functools
import math

import jax
import jax.numpy as jnp
from jax import lax
from jax.experimental import pallas as pl
from jax.experimental.pallas import tpu as pltpu
from jax.sharding import PartitionSpec as P

PARTS = (1, 1, 1, 1, 1, 1, 1, 1)
CHUNKS = 4
DELAY = 3
SMEM = pl.BlockSpec(memory_space=pltpu.SMEM)
VMEM = pl.BlockSpec(memory_space=pltpu.VMEM)
HBM = pl.BlockSpec(memory_space=pltpu.HBM)


def entry_turn(depth):
    return DELAY * depth


def taper_row(block, block_rows, width):
    lateral = block_rows * width
    position = block * width + lax.broadcasted_iota(jnp.int32, (1, width), 1)
    distance = jnp.minimum(position, lateral - 1 - position).astype(jnp.float32)
    edge_ramp = jnp.maximum(0.0, 1.0 - distance / (lateral // 32))
    return 1.0 - 0.3 * edge_ramp * edge_ramp


def split_halves(value):
    high = value.astype(jnp.bfloat16)
    low = (value - high.astype(jnp.float32)).astype(jnp.bfloat16)
    return high, low


def any_of(group, members):
    found = group == members[0]
    for member in members[1:]:
        found = jnp.logical_or(found, group == member)
    return found


def propagate_kernel(*refs, turn, sizes, offsets, classes, arrived, send):
    refs = list(refs)
    first = turn == 0
    if first:
        columns_in, pairs_in, propagator = refs[:3]
        del refs[:3]
    else:
        columns, operator, kept_in = refs[:3]
        del refs[:3]
    arrived = {c: refs.pop(0) for c in arrived}
    surface = [refs.pop(0), refs.pop(0)] if turn < len(sizes) else None
    if first:
        columns, pairs, operator = refs[:3]
        del refs[:3]
    kept = refs.pop(0)
    outs = {c: refs.pop(0) for c in send}
    splits = {c: refs.pop(0) for c in classes}
    if surface:
        drawn, surface_sems = refs[:2]
        del refs[:2]
    block_rows, nnz = operator.shape[:2]
    width = operator.shape[-1]
    depth = lax.axis_index("depth")
    group = turn - entry_turn(depth)

    def chunk(k):
        rows = pl.ds(k * (block_rows // CHUNKS), block_rows // CHUNKS)
        return pltpu.make_async_copy(
            propagator.at[0, 0, rows], operator.at[rows], refs[0].at[k])

    if surface:
        draws = [
            pltpu.make_async_copy(
                surface[k].at[0, :, pl.ds(offsets[turn], sizes[turn]), :],
                drawn.at[k], surface_sems.at[k])
            for k in range(2)
        ]

        @pl.when(depth == 0)
        def _():
            for copy in draws:
                copy.start()

    if first:
        for k in range(CHUNKS):
            chunk(k).start()
        tables = [pltpu.make_async_copy(columns_in, columns, refs[1].at[0]),
                  pltpu.make_async_copy(pairs_in, pairs, refs[1].at[1])]
        for copy in tables:
            copy.start()
        for copy in tables:
            copy.wait()

    def level(shots):
        rows = 2 * shots
        split = splits[shots]
        members = [g for g in range(len(sizes)) if sizes[g] == shots]

        def put(block, part, value):
            high, low = split_halves(value)
            split[block, part * rows:(part + 1) * rows, :] = high
            split[block, (2 + part) * rows:(3 + part) * rows, :] = low

        if surface and sizes[turn] == shots:
            @pl.when(depth == 0)
            def _():
                for copy in draws:
                    copy.wait()
                for block in range(block_rows):
                    lanes = slice(block * width, (block + 1) * width)
                    for part in range(2):
                        receiver = drawn[1, part, :, lanes]
                        if part == 1:
                            receiver = -receiver
                        put(block, part, jnp.concatenate(
                            [drawn[0, part, :, lanes], receiver], axis=0))

        if shots in arrived:
            @pl.when(depth > 0)
            def _():
                for block in range(block_rows):
                    for part in range(2):
                        put(block, part, arrived[shots][block, part])

        start = jnp.int32(0)
        for member in members:
            start = jnp.where(group == member, offsets[member], start)
        start = pl.multiple_of(start, 8)
        place = pl.ds(start, shots)

        for r in range(block_rows):
            if first and r % (block_rows // CHUNKS) == 0:
                chunk(r // (block_rows // CHUNKS)).wait()
            picked = jnp.concatenate(
                [split[columns[j, 0, r]] for j in range(nnz)], axis=1
            )
            real = operator[r, :, 0].reshape(nnz * width, width)
            imag = operator[r, :, 1].reshape(nnz * width, width)
            weights = jnp.concatenate([real, imag], axis=1)
            product = jnp.dot(picked, weights, preferred_element_type=jnp.float32)
            product = product[: 2 * rows] + product[2 * rows:]
            scale = taper_row(r, block_rows, width)
            real_out = (product[:rows, :width] - product[rows:, width:]) * scale
            imag_out = (product[rows:, :width] + product[:rows, width:]) * scale
            for part, value in ((0, real_out), (1, imag_out)):
                if shots in send:
                    outs[shots][r, part] = value
                kept[r, part, 0, place, :] = value[:shots]
                kept[r, part, 1, place, :] = value[shots:]

    for shots in classes:
        members = [g for g in range(len(sizes)) if sizes[g] == shots]
        pl.when(any_of(group, members))(functools.partial(level, shots))

    if first:
        @pl.when(depth > 0)
        def _():
            for k in range(CHUNKS):
                chunk(k).wait()


def image_block(pairs, index, kept, shots, scale):
    a = pairs[0, 0, index]
    b = pairs[0, 1, index]
    left = jnp.concatenate([kept[a, 0, 0, shots, :], kept[a, 1, 0, shots, :]], axis=0) * scale
    right = jnp.concatenate([kept[b, 0, 1, shots, :], -kept[b, 1, 1, shots, :]], axis=0)
    left_high, left_low = split_halves(left)
    right_high, right_low = split_halves(right)
    lhs = jnp.concatenate([left_high, left_high, left_low], axis=0)
    rhs = jnp.concatenate([right_high, right_low, right_high], axis=0)
    return lax.dot_general(
        lhs, rhs, (((0,), (0,)), ((), ())), preferred_element_type=jnp.float32
    )


def early_kernel(pairs, kept_in, kept, out, *, shots, scale):
    for index in range(out.shape[0]):
        out[index] = image_block(pairs, index, kept_in, shots, scale)


def last_kernel(pairs, early, kept, *outs, shots, scale):
    share = outs[0].shape[0]
    parts = len(outs)
    own = lax.axis_index("freq")
    for step in range(parts):
        owner = lax.rem(own + step, parts)
        for index in range(share):
            pair = owner * share + index
            outs[step][index] = early[pair] + image_block(pairs, pair, kept, shots, scale)


def shards(source_field, receiver_data, propagator, block_columns, image_pairs):
    depth_count = lax.axis_size("depth")
    freq_count = lax.axis_size("freq")
    shots_all, lateral = source_field.shape[2:]
    block_rows, nnz = propagator.shape[2:4]
    width = propagator.shape[-1]
    pair_count = image_pairs.shape[1]
    unit = shots_all // sum(PARTS)
    sizes = [unit * part for part in PARTS]
    offsets = [sum(sizes[:g]) for g in range(len(sizes))]
    groups = len(sizes)
    scale = 1.0 / math.sqrt(2.0 * shots_all * freq_count)
    kept_type = pltpu.VMEM((block_rows, 2, 2, shots_all, width), jnp.float32)
    params = pltpu.CompilerParams(vmem_limit_bytes=16 * 1024 * 1024)
    turns = groups + entry_turn(depth_count - 1)

    def hbm(value):
        return pltpu.with_memory_space_constraint(value, pltpu.HBM)

    source_field, receiver_data, propagator = map(hbm, (source_field, receiver_data, propagator))

    def size_of(d, turn):
        group = turn - entry_turn(d)
        return sizes[group] if 0 <= group < groups else None

    sent = {}
    for turn in range(turns):
        arrived = sent.pop(turn - DELAY, {})
        present = [size_of(d, turn) for d in range(depth_count)]
        classes = sorted({c for c in present if c})
        send = sorted({c for c in present[:-1] if c})
        if turn == 0:
            columns_in = hbm(block_columns.transpose(2, 0, 1))
            pairs_in = hbm(image_pairs.transpose(0, 2, 1))
            operands = [columns_in, pairs_in, propagator]
            specs = [HBM, HBM, HBM]
            out_shape = [pltpu.SMEM(columns_in.shape, jnp.int32),
                         pltpu.SMEM(pairs_in.shape, jnp.int32),
                         pltpu.VMEM(propagator.shape[2:], propagator.dtype),
                         kept_type]
            out_specs = [SMEM, SMEM, VMEM, VMEM]
            aliases = {}
        else:
            operands = [columns, operator, kept]
            specs = [SMEM, VMEM, VMEM]
            out_shape = [kept_type]
            out_specs = [VMEM]
            aliases = {2: 0}
        operands += list(arrived.values())
        specs += [VMEM] * len(arrived)
        out_shape += [pltpu.VMEM((block_rows, 2, 2 * c, width), jnp.float32) for c in send]
        out_specs += [VMEM] * len(send)
        scratch = [pltpu.VMEM((block_rows, 8 * c, width), jnp.bfloat16) for c in classes]
        if turn < groups:
            operands += [source_field, receiver_data]
            specs += [HBM, HBM]
            scratch += [pltpu.VMEM((2, 2, sizes[turn], lateral), jnp.float32),
                        pltpu.SemaphoreType.DMA((2,))]
        if turn == 0:
            scratch += [pltpu.SemaphoreType.DMA((CHUNKS,)), pltpu.SemaphoreType.DMA((2,))]
        results = pl.pallas_call(
            functools.partial(
                propagate_kernel, turn=turn, sizes=sizes, offsets=offsets, classes=classes,
                arrived=list(arrived), send=send),
            out_shape=out_shape,
            in_specs=specs,
            out_specs=out_specs,
            input_output_aliases=aliases,
            scratch_shapes=scratch,
            compiler_params=params,
            cost_estimate=pl.CostEstimate(flops=0, bytes_accessed=0, transcendentals=0),
        )(*operands)
        if turn == 0:
            columns, pairs, operator = results[:3]
            results = results[3:]
        kept = results[0]
        fields = dict(zip(send, results[1:]))
        sent[turn] = {
            c: lax.ppermute(fields[c], "depth", [
                (d, d + 1) for d in range(depth_count - 1) if size_of(d, turn) == c])
            for c in send
        }
        if turn == turns - 2:
            image_type = pltpu.VMEM((pair_count, width, width), jnp.float32)
            kept, early = pl.pallas_call(
                functools.partial(early_kernel, shots=slice(0, offsets[-1]), scale=scale),
                out_shape=(kept_type, image_type),
                in_specs=[SMEM, VMEM],
                out_specs=(VMEM, VMEM),
                input_output_aliases={1: 0},
                compiler_params=params,
            )(pairs, kept)

    share = pair_count // freq_count
    share_type = pltpu.VMEM((share, width, width), jnp.float32)
    shares = pl.pallas_call(
        functools.partial(last_kernel, shots=slice(offsets[-1], shots_all), scale=scale),
        out_shape=(share_type,) * freq_count,
        in_specs=[SMEM, VMEM, VMEM],
        out_specs=(VMEM,) * freq_count,
        compiler_params=params,
    )(pairs, early, kept)
    total = shares[0]
    for step in range(1, freq_count):
        total += lax.ppermute(
            shares[step], "freq", [(f, (f + step) % freq_count) for f in range(freq_count)])
    return total[None]


def solution(mesh):
    placed = (
        P("freq", None, None, None),
        P("freq", None, None, None),
        P("freq", "depth", None, None, None, None, None),
        P("depth", None, None),
        P("depth", None, None),
    )
    return jax.shard_map(
        shards,
        mesh=mesh,
        in_specs=placed,
        out_specs=P("depth", "freq", None, None),
        check_vma=False,
    )
```

```python
import functools
import math

import jax
import jax.numpy as jnp
from jax import lax
from jax.experimental import pallas as pl
from jax.experimental.pallas import tpu as pltpu
from jax.sharding import PartitionSpec as P

PARTS = (1, 1, 1, 1, 1, 1, 1, 1)
CHUNKS = 4
DELAY = 3
SMEM = pl.BlockSpec(memory_space=pltpu.SMEM)
VMEM = pl.BlockSpec(memory_space=pltpu.VMEM)
HBM = pl.BlockSpec(memory_space=pltpu.HBM)


def entry_turn(depth):
    return DELAY * depth


def taper_row(block, block_rows, width):
    lateral = block_rows * width
    position = block * width + lax.broadcasted_iota(jnp.int32, (1, width), 1)
    distance = jnp.minimum(position, lateral - 1 - position).astype(jnp.float32)
    edge_ramp = jnp.maximum(0.0, 1.0 - distance / (lateral // 32))
    return 1.0 - 0.3 * edge_ramp * edge_ramp


def split_halves(value):
    high = value.astype(jnp.bfloat16)
    low = (value - high.astype(jnp.float32)).astype(jnp.bfloat16)
    return high, low


def any_of(group, members):
    found = group == members[0]
    for member in members[1:]:
        found = jnp.logical_or(found, group == member)
    return found


def propagate_kernel(*refs, turn, sizes, offsets, classes, arrived, send):
    refs = list(refs)
    first = turn == 0
    if first:
        columns_in, pairs_in, propagator = refs[:3]
        del refs[:3]
    else:
        columns, operator, kept_in = refs[:3]
        del refs[:3]
    arrived = {c: refs.pop(0) for c in arrived}
    drawn = refs.pop(0) if 0 < turn < len(sizes) else None
    surface = [refs.pop(0), refs.pop(0)] if turn + 1 < len(sizes) else None
    if first:
        columns, pairs, operator = refs[:3]
        del refs[:3]
    kept = refs.pop(0)
    upcoming = refs.pop(0) if surface else None
    outs = {c: refs.pop(0) for c in send}
    splits = {c: refs.pop(0) for c in classes}
    if surface:
        surface_sems = refs.pop(0)
    if first:
        drawn = refs.pop(0)
    block_rows, nnz = operator.shape[:2]
    width = operator.shape[-1] // 2
    depth = lax.axis_index("depth")
    group = turn - entry_turn(depth)

    def chunk(k):
        rows = pl.ds(k * (block_rows // CHUNKS), block_rows // CHUNKS)
        return [
            pltpu.make_async_copy(
                propagator.at[0, 0, rows, :, part],
                operator.at[rows, :, :, pl.ds(part * width, width)], refs[0].at[k, part])
            for part in range(2)
        ]

    def draw(g, target, slot):
        return [
            pltpu.make_async_copy(
                surface[k].at[0, :, pl.ds(offsets[g], sizes[g]), :],
                target.at[k], surface_sems.at[slot, k])
            for k in range(2)
        ]

    if first:
        tables = [pltpu.make_async_copy(columns_in, columns, refs[1].at[0]),
                  pltpu.make_async_copy(pairs_in, pairs, refs[1].at[1])]
        for copy in tables:
            copy.start()

        @pl.when(depth == 0)
        def _():
            for copy in draw(0, drawn, 0):
                copy.start()

    if upcoming is not None:
        @pl.when(depth == 0)
        def _():
            for copy in draw(turn + 1, upcoming, 1):
                copy.start()

    if first:
        for k in range(CHUNKS):
            for copy in chunk(k):
                copy.start()
        for copy in tables:
            copy.wait()

    def level(shots):
        rows = 2 * shots
        split = splits[shots]
        members = [g for g in range(len(sizes)) if sizes[g] == shots]

        def put(block, part, value):
            high, low = split_halves(value)
            split[block, part * rows:(part + 1) * rows, :] = high
            split[block, (2 + part) * rows:(3 + part) * rows, :] = low

        if turn < len(sizes) and sizes[turn] == shots:
            @pl.when(depth == 0)
            def _():
                if first:
                    for copy in draw(0, drawn, 0):
                        copy.wait()
                for block in range(block_rows):
                    lanes = slice(block * width, (block + 1) * width)
                    for part in range(2):
                        receiver = drawn[1, part, :, lanes]
                        if part == 1:
                            receiver = -receiver
                        put(block, part, jnp.concatenate(
                            [drawn[0, part, :, lanes], receiver], axis=0))

        if shots in arrived:
            @pl.when(depth > 0)
            def _():
                for block in range(block_rows):
                    for part in range(2):
                        put(block, part, arrived[shots][block, part])

        start = jnp.int32(0)
        for member in members:
            start = jnp.where(group == member, offsets[member], start)
        start = pl.multiple_of(start, 8)
        place = pl.ds(start, shots)

        for r in range(block_rows):
            if first and r % (block_rows // CHUNKS) == 0:
                for copy in chunk(r // (block_rows // CHUNKS)):
                    copy.wait()
            picked = jnp.concatenate(
                [split[columns[j, 0, r]] for j in range(nnz)], axis=1
            )
            weights = operator[r].reshape(nnz * width, 2 * width)
            product = jnp.dot(picked, weights, preferred_element_type=jnp.float32)
            product = product[: 2 * rows] + product[2 * rows:]
            scale = taper_row(r, block_rows, width)
            real_out = (product[:rows, :width] - product[rows:, width:]) * scale
            imag_out = (product[rows:, :width] + product[:rows, width:]) * scale
            for part, value in ((0, real_out), (1, imag_out)):
                if shots in send:
                    outs[shots][r, part] = value
                kept[r, part, 0, place, :] = value[:shots]
                kept[r, part, 1, place, :] = value[shots:]

    for shots in classes:
        members = [g for g in range(len(sizes)) if sizes[g] == shots]
        pl.when(any_of(group, members))(functools.partial(level, shots))

    if first:
        @pl.when(depth > 0)
        def _():
            for k in range(CHUNKS):
                for copy in chunk(k):
                    copy.wait()

    if upcoming is not None:
        @pl.when(depth == 0)
        def _():
            for copy in draw(turn + 1, upcoming, 1):
                copy.wait()


def image_block(pairs, index, kept, shots, scale):
    a = pairs[0, 0, index]
    b = pairs[0, 1, index]
    left = jnp.concatenate([kept[a, 0, 0, shots, :], kept[a, 1, 0, shots, :]], axis=0) * scale
    right = jnp.concatenate([kept[b, 0, 1, shots, :], -kept[b, 1, 1, shots, :]], axis=0)
    left_high, left_low = split_halves(left)
    right_high, right_low = split_halves(right)
    lhs = jnp.concatenate([left_high, left_high, left_low], axis=0)
    rhs = jnp.concatenate([right_high, right_low, right_high], axis=0)
    return lax.dot_general(
        lhs, rhs, (((0,), (0,)), ((), ())), preferred_element_type=jnp.float32
    )


def owned(outs):
    share = outs[0].shape[0]
    parts = len(outs)
    own = lax.axis_index("freq")
    for step in range(parts):
        owner = lax.rem(own + step, parts)
        for index in range(share):
            yield step, index, owner * share + index


def share_kernel(pairs, kept_in, kept, *outs, shots, scale):
    for step, index, pair in owned(outs):
        outs[step][index] = image_block(pairs, pair, kept_in, shots, scale)


def last_kernel(pairs, kept, *refs, shots, scale):
    early, outs = refs[:len(refs) // 2], refs[len(refs) // 2:]
    for step, index, pair in owned(outs):
        outs[step][index] = early[step][index] + image_block(pairs, pair, kept, shots, scale)


def shards(source_field, receiver_data, propagator, block_columns, image_pairs):
    depth_count = lax.axis_size("depth")
    freq_count = lax.axis_size("freq")
    shots_all, lateral = source_field.shape[2:]
    block_rows, nnz = propagator.shape[2:4]
    width = propagator.shape[-1]
    pair_count = image_pairs.shape[1]
    unit = shots_all // sum(PARTS)
    sizes = [unit * part for part in PARTS]
    offsets = [sum(sizes[:g]) for g in range(len(sizes))]
    groups = len(sizes)
    scale = 1.0 / math.sqrt(2.0 * shots_all * freq_count)
    kept_type = pltpu.VMEM((block_rows, 2, 2, shots_all, width), jnp.float32)
    params = pltpu.CompilerParams(vmem_limit_bytes=16 * 1024 * 1024)
    turns = groups + entry_turn(depth_count - 1)

    def hbm(value):
        return pltpu.with_memory_space_constraint(value, pltpu.HBM)

    source_field, receiver_data, propagator = map(hbm, (source_field, receiver_data, propagator))

    def size_of(d, turn):
        group = turn - entry_turn(d)
        return sizes[group] if 0 <= group < groups else None

    share_type = pltpu.VMEM((pair_count // freq_count, width, width), jnp.float32)

    def shares(kept, shots):
        return pl.pallas_call(
            functools.partial(share_kernel, shots=shots, scale=scale),
            out_shape=(kept_type,) + (share_type,) * freq_count,
            in_specs=[SMEM, VMEM],
            out_specs=(VMEM,) * (1 + freq_count),
            input_output_aliases={1: 0},
            compiler_params=params,
        )(pairs, kept)

    sent = {}
    for turn in range(turns):
        arrived = sent.pop(turn - DELAY, {})
        present = [size_of(d, turn) for d in range(depth_count)]
        classes = sorted({c for c in present if c})
        send = sorted({c for c in present[:-1] if c})
        if turn == 0:
            columns_in = hbm(block_columns.transpose(2, 0, 1))
            pairs_in = hbm(image_pairs.transpose(0, 2, 1))
            operands = [columns_in, pairs_in, propagator]
            specs = [HBM, HBM, HBM]
            out_shape = [pltpu.SMEM(columns_in.shape, jnp.int32),
                         pltpu.SMEM(pairs_in.shape, jnp.int32),
                         pltpu.VMEM((block_rows, nnz, width, 2 * width), propagator.dtype),
                         kept_type]
            out_specs = [SMEM, SMEM, VMEM, VMEM]
            aliases = {}
        else:
            operands = [columns, operator, kept]
            specs = [SMEM, VMEM, VMEM]
            out_shape = [kept_type]
            out_specs = [VMEM]
            aliases = {2: 0}
        operands += list(arrived.values())
        specs += [VMEM] * len(arrived)
        if 0 < turn < groups:
            operands.append(drawn)
            specs.append(VMEM)
        if turn + 1 < groups:
            operands += [source_field, receiver_data]
            specs += [HBM, HBM]
            out_shape.append(pltpu.VMEM((2, 2, sizes[turn + 1], lateral), jnp.float32))
            out_specs.append(VMEM)
        out_shape += [pltpu.VMEM((block_rows, 2, 2 * c, width), jnp.float32) for c in send]
        out_specs += [VMEM] * len(send)
        scratch = [pltpu.VMEM((block_rows, 8 * c, width), jnp.bfloat16) for c in classes]
        if turn + 1 < groups:
            scratch += [pltpu.SemaphoreType.DMA((2, 2))]
        if turn == 0:
            scratch += [pltpu.VMEM((2, 2, sizes[0], lateral), jnp.float32),
                        pltpu.SemaphoreType.DMA((CHUNKS, 2)), pltpu.SemaphoreType.DMA((2,))]
        results = pl.pallas_call(
            functools.partial(
                propagate_kernel, turn=turn, sizes=sizes, offsets=offsets, classes=classes,
                arrived=list(arrived), send=send),
            out_shape=out_shape,
            in_specs=specs,
            out_specs=out_specs,
            input_output_aliases=aliases,
            scratch_shapes=scratch,
            compiler_params=params,
            cost_estimate=pl.CostEstimate(flops=0, bytes_accessed=0, transcendentals=0),
        )(*operands)
        if turn == 0:
            columns, pairs, operator = results[:3]
            results = results[3:]
        kept = results[0]
        results = results[1:]
        if turn + 1 < groups:
            drawn = results[0]
            results = results[1:]
        fields = dict(zip(send, results))
        sent[turn] = {
            c: lax.ppermute(fields[c], "depth", [
                (d, d + 1) for d in range(depth_count - 1) if size_of(d, turn) == c])
            for c in send
        }
        if turn == turns - 2:
            kept, *early = shares(kept, slice(0, offsets[-1]))

    lasts = pl.pallas_call(
        functools.partial(last_kernel, shots=slice(offsets[-1], shots_all), scale=scale),
        out_shape=(share_type,) * freq_count,
        in_specs=[SMEM] + [VMEM] * (1 + freq_count),
        out_specs=(VMEM,) * freq_count,
        compiler_params=params,
    )(pairs, kept, *early)
    total = lasts[0]
    for step in sorted(range(1, freq_count), key=lambda step: step % 2):
        total += lax.ppermute(
            lasts[step], "freq", [(f, (f + step) % freq_count) for f in range(freq_count)])
    return total[None]


def solution(mesh):
    placed = (
        P("freq", None, None, None),
        P("freq", None, None, None),
        P("freq", "depth", None, None, None, None, None),
        P("depth", None, None),
        P("depth", None, None),
    )
    return jax.shard_map(
        shards,
        mesh=mesh,
        in_specs=placed,
        out_specs=P("depth", "freq", None, None),
        check_vma=False,
    )
```

```python
import functools
import math

import jax
import jax.numpy as jnp
from jax import lax
from jax.experimental import pallas as pl
from jax.experimental.pallas import tpu as pltpu
from jax.sharding import PartitionSpec as P

PARTS = (1, 1, 1, 1, 1, 1, 1, 1)
CHUNKS = 4
DELAY = 3
SMEM = pl.BlockSpec(memory_space=pltpu.SMEM)
VMEM = pl.BlockSpec(memory_space=pltpu.VMEM)
HBM = pl.BlockSpec(memory_space=pltpu.HBM)


def entry_turn(depth):
    return DELAY * depth


def taper_row(block, block_rows, width):
    lateral = block_rows * width
    position = block * width + lax.broadcasted_iota(jnp.int32, (1, width), 1)
    distance = jnp.minimum(position, lateral - 1 - position).astype(jnp.float32)
    edge_ramp = jnp.maximum(0.0, 1.0 - distance / (lateral // 32))
    return 1.0 - 0.3 * edge_ramp * edge_ramp


def split_halves(value):
    high = value.astype(jnp.bfloat16)
    low = (value - high.astype(jnp.float32)).astype(jnp.bfloat16)
    return high, low


def any_of(group, members):
    found = group == members[0]
    for member in members[1:]:
        found = jnp.logical_or(found, group == member)
    return found


def propagate_kernel(*refs, turn, sizes, offsets, classes, arrived, send):
    refs = list(refs)
    first = turn == 0
    if first:
        columns_in, pairs_in, propagator = refs[:3]
        del refs[:3]
    else:
        columns, operator, kept_in = refs[:3]
        del refs[:3]
    arrived = {c: refs.pop(0) for c in arrived}
    drawn = refs.pop(0) if 0 < turn < len(sizes) else None
    surface = [refs.pop(0), refs.pop(0)] if turn + 1 < len(sizes) else None
    if first:
        columns, pairs, operator = refs[:3]
        del refs[:3]
    kept = refs.pop(0)
    upcoming = refs.pop(0) if surface else None
    outs = {c: refs.pop(0) for c in send}
    splits = {c: refs.pop(0) for c in classes}
    if surface:
        surface_sems = refs.pop(0)
    if first:
        drawn = refs.pop(0)
    block_rows, nnz = operator.shape[:2]
    width = operator.shape[-1] // 2
    depth = lax.axis_index("depth")
    group = turn - entry_turn(depth)

    def chunk(k):
        rows = pl.ds(k * (block_rows // CHUNKS), block_rows // CHUNKS)
        return [
            pltpu.make_async_copy(
                propagator.at[0, 0, rows, :, part],
                operator.at[rows, :, :, pl.ds(part * width, width)], refs[0].at[k, part])
            for part in range(2)
        ]

    def draw(g, target, slot):
        return [
            pltpu.make_async_copy(
                surface[k].at[0, :, pl.ds(offsets[g], sizes[g]), :],
                target.at[k], surface_sems.at[slot, k])
            for k in range(2)
        ]

    if first:
        tables = [pltpu.make_async_copy(columns_in, columns, refs[1].at[0]),
                  pltpu.make_async_copy(pairs_in, pairs, refs[1].at[1])]
        for copy in tables:
            copy.start()

        @pl.when(depth == 0)
        def _():
            for copy in draw(0, drawn, 0):
                copy.start()

    if upcoming is not None:
        @pl.when(depth == 0)
        def _():
            for copy in draw(turn + 1, upcoming, 1):
                copy.start()

    if first:
        for k in range(CHUNKS):
            for copy in chunk(k):
                copy.start()
        for copy in tables:
            copy.wait()

    def level(shots):
        rows = 2 * shots
        split = splits[shots]
        members = [g for g in range(len(sizes)) if sizes[g] == shots]

        def put(block, part, value):
            high, low = split_halves(value)
            split[block, part * rows:(part + 1) * rows, :] = high
            split[block, (2 + part) * rows:(3 + part) * rows, :] = low

        if turn < len(sizes) and sizes[turn] == shots:
            @pl.when(depth == 0)
            def _():
                if first:
                    for copy in draw(0, drawn, 0):
                        copy.wait()
                for block in range(block_rows):
                    lanes = slice(block * width, (block + 1) * width)
                    for part in range(2):
                        receiver = drawn[1, part, :, lanes]
                        if part == 1:
                            receiver = -receiver
                        put(block, part, jnp.concatenate(
                            [drawn[0, part, :, lanes], receiver], axis=0))

        if shots in arrived:
            @pl.when(depth > 0)
            def _():
                for block in range(block_rows):
                    for part in range(2):
                        put(block, part, arrived[shots][block, part])

        start = jnp.int32(0)
        for member in members:
            start = jnp.where(group == member, offsets[member], start)
        start = pl.multiple_of(start, 8)
        place = pl.ds(start, shots)

        for r in range(block_rows):
            if first and r % (block_rows // CHUNKS) == 0:
                for copy in chunk(r // (block_rows // CHUNKS)):
                    copy.wait()
            picked = jnp.concatenate(
                [split[columns[j, 0, r]] for j in range(nnz)], axis=1
            )
            weights = operator[r].reshape(nnz * width, 2 * width)
            product = jnp.dot(picked, weights, preferred_element_type=jnp.float32)
            product = product[: 2 * rows] + product[2 * rows:]
            scale = taper_row(r, block_rows, width)
            real_out = (product[:rows, :width] - product[rows:, width:]) * scale
            imag_out = (product[rows:, :width] + product[:rows, width:]) * scale
            for part, value in ((0, real_out), (1, imag_out)):
                if shots in send:
                    outs[shots][r, part] = value
                kept[r, part, 0, place, :] = value[:shots]
                kept[r, part, 1, place, :] = value[shots:]

    for shots in classes:
        members = [g for g in range(len(sizes)) if sizes[g] == shots]
        pl.when(any_of(group, members))(functools.partial(level, shots))

    if first:
        @pl.when(depth > 0)
        def _():
            for k in range(CHUNKS):
                for copy in chunk(k):
                    copy.wait()

    if upcoming is not None:
        @pl.when(depth == 0)
        def _():
            for copy in draw(turn + 1, upcoming, 1):
                copy.wait()


def image_block(pairs, index, kept, shots, scale):
    a = pairs[0, 0, index]
    b = pairs[0, 1, index]
    left = jnp.concatenate([kept[a, 0, 0, shots, :], kept[a, 1, 0, shots, :]], axis=0) * scale
    right = jnp.concatenate([kept[b, 0, 1, shots, :], -kept[b, 1, 1, shots, :]], axis=0)
    left_high, left_low = split_halves(left)
    right_high, right_low = split_halves(right)
    lhs = jnp.concatenate([left_high, left_high, left_low], axis=0)
    rhs = jnp.concatenate([right_high, right_low, right_high], axis=0)
    return lax.dot_general(
        lhs, rhs, (((0,), (0,)), ((), ())), preferred_element_type=jnp.float32
    )


def owned(outs):
    share = outs[0].shape[0]
    parts = len(outs)
    own = lax.axis_index("freq")
    for step in range(parts):
        owner = lax.rem(own + step, parts)
        for index in range(share):
            yield step, index, owner * share + index


def share_kernel(pairs, kept_in, kept, *outs, shots, scale):
    for step, index, pair in owned(outs):
        outs[step][index] = image_block(pairs, pair, kept_in, shots, scale)


def last_kernel(pairs, kept, *refs, shots, scale):
    early, outs = refs[:len(refs) // 2], refs[len(refs) // 2:]
    for step, index, pair in owned(outs):
        outs[step][index] = early[step][index] + image_block(pairs, pair, kept, shots, scale)


def shards(source_field, receiver_data, propagator, block_columns, image_pairs):
    depth_count = lax.axis_size("depth")
    freq_count = lax.axis_size("freq")
    shots_all, lateral = source_field.shape[2:]
    block_rows, nnz = propagator.shape[2:4]
    width = propagator.shape[-1]
    pair_count = image_pairs.shape[1]
    unit = shots_all // sum(PARTS)
    sizes = [unit * part for part in PARTS]
    offsets = [sum(sizes[:g]) for g in range(len(sizes))]
    groups = len(sizes)
    scale = 1.0 / math.sqrt(2.0 * shots_all * freq_count)
    kept_type = pltpu.VMEM((block_rows, 2, 2, shots_all, width), jnp.float32)
    params = pltpu.CompilerParams(vmem_limit_bytes=16 * 1024 * 1024)
    turns = groups + entry_turn(depth_count - 1)

    def hbm(value):
        return pltpu.with_memory_space_constraint(value, pltpu.HBM)

    source_field, receiver_data, propagator = map(hbm, (source_field, receiver_data, propagator))

    def size_of(d, turn):
        group = turn - entry_turn(d)
        return sizes[group] if 0 <= group < groups else None

    share_type = pltpu.VMEM((pair_count // freq_count, width, width), jnp.float32)

    def shares(kept, shots):
        return pl.pallas_call(
            functools.partial(share_kernel, shots=shots, scale=scale),
            out_shape=(kept_type,) + (share_type,) * freq_count,
            in_specs=[SMEM, VMEM],
            out_specs=(VMEM,) * (1 + freq_count),
            input_output_aliases={1: 0},
            compiler_params=params,
        )(pairs, kept)

    sent = {}
    for turn in range(turns):
        arrived = sent.pop(turn - DELAY, {})
        present = [size_of(d, turn) for d in range(depth_count)]
        classes = sorted({c for c in present if c})
        send = sorted({c for c in present[:-1] if c})
        if turn == 0:
            columns_in = hbm(block_columns.transpose(2, 0, 1))
            pairs_in = hbm(image_pairs.transpose(0, 2, 1))
            operands = [columns_in, pairs_in, propagator]
            specs = [HBM, HBM, HBM]
            out_shape = [pltpu.SMEM(columns_in.shape, jnp.int32),
                         pltpu.SMEM(pairs_in.shape, jnp.int32),
                         pltpu.VMEM((block_rows, nnz, width, 2 * width), propagator.dtype),
                         kept_type]
            out_specs = [SMEM, SMEM, VMEM, VMEM]
            aliases = {}
        else:
            operands = [columns, operator, kept]
            specs = [SMEM, VMEM, VMEM]
            out_shape = [kept_type]
            out_specs = [VMEM]
            aliases = {2: 0}
        operands += list(arrived.values())
        specs += [VMEM] * len(arrived)
        if 0 < turn < groups:
            operands.append(drawn)
            specs.append(VMEM)
        if turn + 1 < groups:
            operands += [source_field, receiver_data]
            specs += [HBM, HBM]
            out_shape.append(pltpu.VMEM((2, 2, sizes[turn + 1], lateral), jnp.float32))
            out_specs.append(VMEM)
        out_shape += [pltpu.VMEM((block_rows, 2, 2 * c, width), jnp.float32) for c in send]
        out_specs += [VMEM] * len(send)
        scratch = [pltpu.VMEM((block_rows, 8 * c, width), jnp.bfloat16) for c in classes]
        if turn + 1 < groups:
            scratch += [pltpu.SemaphoreType.DMA((2, 2))]
        if turn == 0:
            scratch += [pltpu.VMEM((2, 2, sizes[0], lateral), jnp.float32),
                        pltpu.SemaphoreType.DMA((CHUNKS, 2)), pltpu.SemaphoreType.DMA((2,))]
        results = pl.pallas_call(
            functools.partial(
                propagate_kernel, turn=turn, sizes=sizes, offsets=offsets, classes=classes,
                arrived=list(arrived), send=send),
            out_shape=out_shape,
            in_specs=specs,
            out_specs=out_specs,
            input_output_aliases=aliases,
            scratch_shapes=scratch,
            compiler_params=params,
            cost_estimate=pl.CostEstimate(flops=0, bytes_accessed=0, transcendentals=0),
        )(*operands)
        if turn == 0:
            columns, pairs, operator = results[:3]
            results = results[3:]
        kept = results[0]
        results = results[1:]
        if turn + 1 < groups:
            drawn = results[0]
            results = results[1:]
        fields = dict(zip(send, results))
        sent[turn] = {
            c: lax.ppermute(fields[c], "depth", [
                (d, d + 1) for d in range(depth_count - 1) if size_of(d, turn) == c])
            for c in send
        }
        if turn == turns - 2:
            kept, *early = shares(kept, slice(0, offsets[-1]))

    lasts = pl.pallas_call(
        functools.partial(last_kernel, shots=slice(offsets[-1], shots_all), scale=scale),
        out_shape=(share_type,) * freq_count,
        in_specs=[SMEM] + [VMEM] * (1 + freq_count),
        out_specs=(VMEM,) * freq_count,
        compiler_params=params,
    )(pairs, kept, *early)
    total = lasts[0]
    for step in range(1, freq_count):
        total += lax.ppermute(
            lasts[step], "freq", [(f, (f + step) % freq_count) for f in range(freq_count)])
    return total[None]


def solution(mesh):
    placed = (
        P("freq", None, None, None),
        P("freq", None, None, None),
        P("freq", "depth", None, None, None, None, None),
        P("depth", None, None),
        P("depth", None, None),
    )
    return jax.shard_map(
        shards,
        mesh=mesh,
        in_specs=placed,
        out_specs=P("depth", "freq", None, None),
        check_vma=False,
    )
```

```python
import functools
import math

import jax
import jax.numpy as jnp
from jax import lax
from jax.experimental import pallas as pl
from jax.experimental.pallas import tpu as pltpu
from jax.sharding import PartitionSpec as P

PARTS = (1, 1, 1, 1, 1, 1, 1, 1)
CHUNKS = 4
DELAY = 3
SMEM = pl.BlockSpec(memory_space=pltpu.SMEM)
VMEM = pl.BlockSpec(memory_space=pltpu.VMEM)
HBM = pl.BlockSpec(memory_space=pltpu.HBM)


def entry_turn(depth):
    return DELAY * depth


def taper_row(block, block_rows, width):
    lateral = block_rows * width
    position = block * width + lax.broadcasted_iota(jnp.int32, (1, width), 1)
    distance = jnp.minimum(position, lateral - 1 - position).astype(jnp.float32)
    edge_ramp = jnp.maximum(0.0, 1.0 - distance / (lateral // 32))
    return 1.0 - 0.3 * edge_ramp * edge_ramp


def split_halves(value):
    high = value.astype(jnp.bfloat16)
    low = (value - high.astype(jnp.float32)).astype(jnp.bfloat16)
    return high, low


def any_of(group, members):
    found = group == members[0]
    for member in members[1:]:
        found = jnp.logical_or(found, group == member)
    return found


def propagate_kernel(*refs, turn, sizes, offsets, classes, arrived, send):
    refs = list(refs)
    first = turn == 0
    if first:
        columns_in, pairs_in, propagator = refs[:3]
        del refs[:3]
    else:
        columns, operator, kept_in = refs[:3]
        del refs[:3]
    arrived = {c: refs.pop(0) for c in arrived}
    drawn = refs.pop(0) if 0 < turn < len(sizes) else None
    surface = [refs.pop(0), refs.pop(0)] if turn + 1 < len(sizes) else None
    if first:
        columns, pairs, operator = refs[:3]
        del refs[:3]
    kept = refs.pop(0)
    upcoming = refs.pop(0) if surface else None
    outs = {c: refs.pop(0) for c in send}
    splits = {c: refs.pop(0) for c in classes}
    if surface:
        surface_sems = refs.pop(0)
    if first:
        drawn = refs.pop(0)
    block_rows, nnz = operator.shape[:2]
    width = operator.shape[-1] // 2
    depth = lax.axis_index("depth")
    group = turn - entry_turn(depth)

    def chunk(k):
        rows = pl.ds(k * (block_rows // CHUNKS), block_rows // CHUNKS)
        return [
            pltpu.make_async_copy(
                propagator.at[0, 0, rows, :, part],
                operator.at[rows, :, :, pl.ds(part * width, width)], refs[0].at[k, part])
            for part in range(2)
        ]

    def draw(g, target, slot):
        return [
            pltpu.make_async_copy(
                surface[k].at[0, :, pl.ds(offsets[g], sizes[g]), :],
                target.at[k], surface_sems.at[slot, k])
            for k in range(2)
        ]

    if first:
        tables = [pltpu.make_async_copy(columns_in, columns, refs[1].at[0]),
                  pltpu.make_async_copy(pairs_in, pairs, refs[1].at[1])]
        for copy in tables:
            copy.start()

        @pl.when(depth == 0)
        def _():
            for copy in draw(0, drawn, 0):
                copy.start()

    if first:
        for k in range(CHUNKS):
            for part, copy in enumerate(chunk(k)):
                copy.start(priority=part)

    if upcoming is not None:
        @pl.when(depth == 0)
        def _():
            for copy in draw(turn + 1, upcoming, 1):
                copy.start()

    if first:
        for copy in tables:
            copy.wait()

    def level(shots):
        rows = 2 * shots
        split = splits[shots]
        members = [g for g in range(len(sizes)) if sizes[g] == shots]

        def put(block, part, value):
            high, low = split_halves(value)
            split[block, part * rows:(part + 1) * rows, :] = high
            split[block, (2 + part) * rows:(3 + part) * rows, :] = low

        if turn < len(sizes) and sizes[turn] == shots:
            @pl.when(depth == 0)
            def _():
                if first:
                    for copy in draw(0, drawn, 0):
                        copy.wait()
                for block in range(block_rows):
                    lanes = slice(block * width, (block + 1) * width)
                    for part in range(2):
                        receiver = drawn[1, part, :, lanes]
                        if part == 1:
                            receiver = -receiver
                        put(block, part, jnp.concatenate(
                            [drawn[0, part, :, lanes], receiver], axis=0))

        if shots in arrived:
            @pl.when(depth > 0)
            def _():
                for block in range(block_rows):
                    for part in range(2):
                        put(block, part, arrived[shots][block, part])

        start = jnp.int32(0)
        for member in members:
            start = jnp.where(group == member, offsets[member], start)
        start = pl.multiple_of(start, 8)
        place = pl.ds(start, shots)

        for r in range(block_rows):
            if first and r % (block_rows // CHUNKS) == 0:
                for copy in chunk(r // (block_rows // CHUNKS)):
                    copy.wait()
            picked = jnp.concatenate(
                [split[columns[j, 0, r]] for j in range(nnz)], axis=1
            )
            weights = operator[r].reshape(nnz * width, 2 * width)
            product = jnp.dot(picked, weights, preferred_element_type=jnp.float32)
            product = product[: 2 * rows] + product[2 * rows:]
            scale = taper_row(r, block_rows, width)
            real_out = (product[:rows, :width] - product[rows:, width:]) * scale
            imag_out = (product[rows:, :width] + product[:rows, width:]) * scale
            for part, value in ((0, real_out), (1, imag_out)):
                if shots in send:
                    outs[shots][r, part] = value
                kept[r, part, 0, place, :] = value[:shots]
                kept[r, part, 1, place, :] = value[shots:]

    for shots in classes:
        members = [g for g in range(len(sizes)) if sizes[g] == shots]
        pl.when(any_of(group, members))(functools.partial(level, shots))

    if first:
        @pl.when(depth > 0)
        def _():
            for k in range(CHUNKS):
                for copy in chunk(k):
                    copy.wait()

    if upcoming is not None:
        @pl.when(depth == 0)
        def _():
            for copy in draw(turn + 1, upcoming, 1):
                copy.wait()


def image_block(pairs, index, kept, shots, scale):
    a = pairs[0, 0, index]
    b = pairs[0, 1, index]
    left = jnp.concatenate([kept[a, 0, 0, shots, :], kept[a, 1, 0, shots, :]], axis=0) * scale
    right = jnp.concatenate([kept[b, 0, 1, shots, :], -kept[b, 1, 1, shots, :]], axis=0)
    left_high, left_low = split_halves(left)
    right_high, right_low = split_halves(right)
    lhs = jnp.concatenate([left_high, left_high, left_low], axis=0)
    rhs = jnp.concatenate([right_high, right_low, right_high], axis=0)
    return lax.dot_general(
        lhs, rhs, (((0,), (0,)), ((), ())), preferred_element_type=jnp.float32
    )


def owned(outs):
    share = outs[0].shape[0]
    parts = len(outs)
    own = lax.axis_index("freq")
    for step in range(parts):
        owner = lax.rem(own + step, parts)
        for index in range(share):
            yield step, index, owner * share + index


def share_kernel(pairs, kept_in, kept, *outs, shots, scale):
    for step, index, pair in owned(outs):
        outs[step][index] = image_block(pairs, pair, kept_in, shots, scale)


def last_kernel(pairs, kept, *refs, shots, scale):
    early, outs = refs[:len(refs) // 2], refs[len(refs) // 2:]
    for step, index, pair in owned(outs):
        outs[step][index] = early[step][index] + image_block(pairs, pair, kept, shots, scale)


def shards(source_field, receiver_data, propagator, block_columns, image_pairs):
    depth_count = lax.axis_size("depth")
    freq_count = lax.axis_size("freq")
    shots_all, lateral = source_field.shape[2:]
    block_rows, nnz = propagator.shape[2:4]
    width = propagator.shape[-1]
    pair_count = image_pairs.shape[1]
    unit = shots_all // sum(PARTS)
    sizes = [unit * part for part in PARTS]
    offsets = [sum(sizes[:g]) for g in range(len(sizes))]
    groups = len(sizes)
    scale = 1.0 / math.sqrt(2.0 * shots_all * freq_count)
    kept_type = pltpu.VMEM((block_rows, 2, 2, shots_all, width), jnp.float32)
    params = pltpu.CompilerParams(vmem_limit_bytes=16 * 1024 * 1024)
    turns = groups + entry_turn(depth_count - 1)

    def hbm(value):
        return pltpu.with_memory_space_constraint(value, pltpu.HBM)

    source_field, receiver_data, propagator = map(hbm, (source_field, receiver_data, propagator))

    def size_of(d, turn):
        group = turn - entry_turn(d)
        return sizes[group] if 0 <= group < groups else None

    share_type = pltpu.VMEM((pair_count // freq_count, width, width), jnp.float32)

    def shares(kept, shots):
        return pl.pallas_call(
            functools.partial(share_kernel, shots=shots, scale=scale),
            out_shape=(kept_type,) + (share_type,) * freq_count,
            in_specs=[SMEM, VMEM],
            out_specs=(VMEM,) * (1 + freq_count),
            input_output_aliases={1: 0},
            compiler_params=params,
        )(pairs, kept)

    sent = {}
    for turn in range(turns):
        arrived = sent.pop(turn - DELAY, {})
        present = [size_of(d, turn) for d in range(depth_count)]
        classes = sorted({c for c in present if c})
        send = sorted({c for c in present[:-1] if c})
        if turn == 0:
            columns_in = hbm(block_columns.transpose(2, 0, 1))
            pairs_in = hbm(image_pairs.transpose(0, 2, 1))
            operands = [columns_in, pairs_in, propagator]
            specs = [HBM, HBM, HBM]
            out_shape = [pltpu.SMEM(columns_in.shape, jnp.int32),
                         pltpu.SMEM(pairs_in.shape, jnp.int32),
                         pltpu.VMEM((block_rows, nnz, width, 2 * width), propagator.dtype),
                         kept_type]
            out_specs = [SMEM, SMEM, VMEM, VMEM]
            aliases = {}
        else:
            operands = [columns, operator, kept]
            specs = [SMEM, VMEM, VMEM]
            out_shape = [kept_type]
            out_specs = [VMEM]
            aliases = {2: 0}
        operands += list(arrived.values())
        specs += [VMEM] * len(arrived)
        if 0 < turn < groups:
            operands.append(drawn)
            specs.append(VMEM)
        if turn + 1 < groups:
            operands += [source_field, receiver_data]
            specs += [HBM, HBM]
            out_shape.append(pltpu.VMEM((2, 2, sizes[turn + 1], lateral), jnp.float32))
            out_specs.append(VMEM)
        out_shape += [pltpu.VMEM((block_rows, 2, 2 * c, width), jnp.float32) for c in send]
        out_specs += [VMEM] * len(send)
        scratch = [pltpu.VMEM((block_rows, 8 * c, width), jnp.bfloat16) for c in classes]
        if turn + 1 < groups:
            scratch += [pltpu.SemaphoreType.DMA((2, 2))]
        if turn == 0:
            scratch += [pltpu.VMEM((2, 2, sizes[0], lateral), jnp.float32),
                        pltpu.SemaphoreType.DMA((CHUNKS, 2)), pltpu.SemaphoreType.DMA((2,))]
        results = pl.pallas_call(
            functools.partial(
                propagate_kernel, turn=turn, sizes=sizes, offsets=offsets, classes=classes,
                arrived=list(arrived), send=send),
            out_shape=out_shape,
            in_specs=specs,
            out_specs=out_specs,
            input_output_aliases=aliases,
            scratch_shapes=scratch,
            compiler_params=params,
            cost_estimate=pl.CostEstimate(flops=0, bytes_accessed=0, transcendentals=0),
        )(*operands)
        if turn == 0:
            columns, pairs, operator = results[:3]
            results = results[3:]
        kept = results[0]
        results = results[1:]
        if turn + 1 < groups:
            drawn = results[0]
            results = results[1:]
        fields = dict(zip(send, results))
        sent[turn] = {
            c: lax.ppermute(fields[c], "depth", [
                (d, d + 1) for d in range(depth_count - 1) if size_of(d, turn) == c])
            for c in send
        }
        if turn == turns - 2:
            kept, *early = shares(kept, slice(0, offsets[-1]))

    lasts = pl.pallas_call(
        functools.partial(last_kernel, shots=slice(offsets[-1], shots_all), scale=scale),
        out_shape=(share_type,) * freq_count,
        in_specs=[SMEM] + [VMEM] * (1 + freq_count),
        out_specs=(VMEM,) * freq_count,
        compiler_params=params,
    )(pairs, kept, *early)
    total = lasts[0]
    for step in range(1, freq_count):
        total += lax.ppermute(
            lasts[step], "freq", [(f, (f + step) % freq_count) for f in range(freq_count)])
    return total[None]


def solution(mesh):
    placed = (
        P("freq", None, None, None),
        P("freq", None, None, None),
        P("freq", "depth", None, None, None, None, None),
        P("depth", None, None),
        P("depth", None, None),
    )
    return jax.shard_map(
        shards,
        mesh=mesh,
        in_specs=placed,
        out_specs=P("depth", "freq", None, None),
        check_vma=False,
    )
```
